32 devices in a mesh: clip: 1, head: 16 (over z, y, x), kv: 2 (over core).
Axes of the slice: x: 2, y: 2, z: 4, core: 2. Of those that a mesh axis runs over, the one named last changes fastest.
Arguments:
- queries: bfloat16 [4096, 4096], P(('clip', 'head')), may hold values from -7 to 7
- keys: bfloat16 [8192, 4096], P(('clip', 'head', 'kv')), may hold values from -5 to 5
- values: bfloat16 [8192, 4096], P(('clip', 'head', 'kv')), may hold values from -6 to 6
- tile_list: int32 [32, 32], P('clip'), may hold values from 0 to 63, as said below
Outputs:
- attended: bfloat16 [4096, 4096], P(('clip', 'head', 'kv'))
The draws below stay inside these ranges and needn't reach their ends.
Inputs may be any that keep to these rules, and one draw needn't show every extreme that they name: `tile_list`: each row names 32 different key tiles. Calling a tile t even when (t // 2) is even, a row names at most 20 even tiles and at most 20 others; some row names exactly 20 even tiles and some row exactly 20 others, in every draw.
All inputs are finite; a program needn't handle non-finite values.
Results may differ from the reference program's by a relative error of at most 0.014.
Values may be sent and summed in bfloat16 or wider, within the bound.
A program may use at most 128 MiB of HBM per device.

```python
import jax
import jax.numpy as jnp
from jax import lax

HEADS = 32
DH = 128
TILE = 128
NSEL = 32
LMAX = 20
KTOK_DEV = 256
SQ = 4096
SK = 8192
QTILES = 32
KTILES = 64


def spike_signs(key):
    coins = jax.random.bernoulli(jax.random.fold_in(key, 91), 0.5, (HEADS * DH,))
    return jnp.where(coins, 1.0, -1.0).astype(jnp.float32)


def draw_queries(key, part):
    base_key = jax.random.fold_in(key, 1)
    drawn = jnp.clip(jax.random.normal(base_key, (SQ, HEADS * DH), jnp.float32), -5.0, 5.0)
    token_pos = jnp.arange(SQ)
    widen = jnp.sqrt(jnp.float32(128.0) / jnp.float32(DH))
    strength = (3.0 + 2.0 * (token_pos // TILE % 3)).astype(jnp.float32) * widen
    spiked = strength[:, None] * spike_signs(key)[None, :]
    return jnp.where((token_pos % TILE == 0)[:, None], spiked, drawn).astype(jnp.bfloat16)


def draw_keys(key, part):
    base_key = jax.random.fold_in(key, 2)
    drawn = jnp.clip(jax.random.normal(base_key, (SK, HEADS * DH), jnp.float32), -5.0, 5.0)
    token_pos = jnp.arange(SK)
    signs = spike_signs(key)[None, :]
    drawn = jnp.where((token_pos % TILE == 0)[:, None], 3.0 * signs, drawn)
    return jnp.where((token_pos % TILE == 1)[:, None], 2.96875 * signs, drawn).astype(jnp.bfloat16)


def draw_tile_list(key, part):
    key_one, key_two, key_three = jax.random.split(key, 3)
    query_pos = jnp.arange(QTILES, dtype=jnp.int32)
    key_pos = jnp.arange(KTILES, dtype=jnp.int32)
    center = (KTILES - QTILES) // 2 + query_pos
    distance = jnp.abs(key_pos[None, :] - center[:, None])
    noise = jax.random.randint(key_one, (QTILES, KTILES), 0, 2 ** 20)
    priority = noise // (1 + distance) * KTILES + key_pos[None, :]
    parity = key_pos // (KTOK_DEV // TILE) % 2
    even_score = jnp.where(parity[None, :] == 0, priority, -1)
    odd_score = jnp.where(parity[None, :] == 1, priority, -1)
    even_top = jax.lax.top_k(even_score, KTILES // 2)[1].astype(jnp.int32)
    odd_top = jax.lax.top_k(odd_score, KTILES // 2)[1].astype(jnp.int32)
    even_count = jax.random.randint(key_two, (QTILES,), NSEL - LMAX, LMAX + 1)
    picked = jax.random.permutation(key_three, QTILES)
    even_count = even_count.at[picked[0]].set(LMAX).at[picked[1]].set(NSEL - LMAX)
    slot_pos = jnp.arange(NSEL, dtype=jnp.int32)[None, :]
    from_even = slot_pos < even_count[:, None]
    even_pick = jnp.take_along_axis(even_top, jnp.broadcast_to(slot_pos, (QTILES, NSEL)), axis=1)
    odd_slot = jnp.clip(slot_pos - even_count[:, None], 0, NSEL - 1)
    odd_pick = jnp.take_along_axis(odd_top, odd_slot, axis=1)
    return jnp.where(from_even, even_pick, odd_pick).astype(jnp.int32)


def steps_of(own_key, extent, shards, low, high):
    gain, own = 1.0, jax.random.fold_in(own_key, 6)
    for dim, shards_of in shards:
        steps = jnp.exp(jax.random.uniform(jax.random.fold_in(own, dim), (shards_of,), jnp.float32, low / len(shards), high / len(shards)))
        gain = gain * jnp.repeat(steps, extent[dim] // shards_of).reshape([-1 if axis == dim else 1 for axis in range(len(extent))])
    return gain


def bell_draw(rng, dims, scale, limit, pieces=(), held_as=jnp.bfloat16):
    factor_of = steps_of(rng, dims, pieces, -0.22, 0.18) if pieces else 1.0
    values = jax.random.normal(rng, dims, jnp.float32) * scale * factor_of
    return jnp.minimum(jnp.maximum(values, -limit), limit).astype(held_as)


def setup_inputs(seed: int = 0, part: int = 0) -> dict:
    arg_keys = jax.random.split(jax.random.key(seed), 5)
    part_keys = jax.random.split(jax.random.fold_in(arg_keys[4], part), 5)
    queries = draw_queries(jax.random.fold_in(jax.random.fold_in(arg_keys[4], part), 71), part)
    keys = draw_keys(jax.random.fold_in(jax.random.fold_in(arg_keys[4], part), 71), part)
    values = bell_draw(part_keys[2], (SK, HEADS * DH), 1.0, 6.0, ((0, 32),))
    tile_list = draw_tile_list(jax.random.fold_in(jax.random.fold_in(arg_keys[4], part), 71), part)
    return {"queries": queries, "keys": keys, "values": values, "tile_list": tile_list}


def reference(queries, keys, values, tile_list):
    inv_root = 1.0 / jnp.sqrt(jnp.float32(DH))
    key_tiles = keys.reshape(KTILES, TILE, HEADS, DH)
    value_tiles = values.reshape(KTILES, TILE, HEADS, DH)

    def one_tile(tile_index):
        query_rows = lax.dynamic_slice_in_dim(queries, tile_index * TILE, TILE, 0)
        query_rows = query_rows.reshape(TILE, HEADS, DH).astype(jnp.float32)
        chosen = tile_list[tile_index]
        key_block = key_tiles[chosen].reshape(NSEL * TILE, HEADS, DH).astype(jnp.float32)
        value_block = value_tiles[chosen].reshape(NSEL * TILE, HEADS, DH).astype(jnp.float32)
        scores = jnp.einsum('qhd,khd->hqk', query_rows, key_block) * inv_root
        row_peak = lax.optimization_barrier(jnp.max(scores, axis=-1, keepdims=True))
        exponent = jnp.exp(scores - row_peak)
        row_total = lax.optimization_barrier(jnp.sum(exponent, axis=-1))
        weight = lax.optimization_barrier(exponent.astype(jnp.bfloat16)).astype(jnp.float32)
        weighted = jnp.einsum('hqk,khd->qhd', weight, value_block)
        result = weighted / row_total.T[:, :, None]
        return result.reshape(TILE, HEADS * DH).astype(jnp.bfloat16)
    result_tiles = lax.map(one_tile, jnp.arange(QTILES, dtype=jnp.int32))
    return result_tiles.reshape(SQ, HEADS * DH)
```

```python
import functools
import math

import jax
import jax.numpy as jnp
from jax import lax
from jax.experimental import pallas as pl
from jax.experimental.pallas import tpu as pltpu
from jax.sharding import PartitionSpec as P

HEADS = 32
DH = 128
TILE = 128
KTOK_DEV = 256
EXP2_SCALE = math.log2(math.e) / math.sqrt(DH)


def general_plan(queries, keys, values, tile_list):
    n_head = lax.axis_size("head")
    heads_dev = HEADS // n_head
    kv_index = lax.axis_index("kv")
    key_all, value_all = (
        lax.all_to_all(keys, "head", split_axis=1, concat_axis=0, tiled=True),
        lax.all_to_all(values, "head", split_axis=1, concat_axis=0, tiled=True),
    )
    tile_span = KTOK_DEV // TILE
    key_shard = tile_list // tile_span
    parity = key_shard % 2
    local_tile = key_shard // 2 * tile_span + tile_list % tile_span
    inv_root = 1.0 / jnp.sqrt(jnp.float32(DH))
    feat_width = key_all.shape[1]
    half_rows = queries.shape[0] // 2
    own_rows = lax.dynamic_slice_in_dim(queries, kv_index * half_rows, half_rows, 0)
    query_part = lax.all_to_all(own_rows, "head", split_axis=1, concat_axis=0, tiled=True)
    key_source, value_source = (
        lax.all_gather(key_all, "kv", axis=0, tiled=True),
        lax.all_gather(value_all, "kv", axis=0, tiled=True),
    )
    full_tile = parity * (key_all.shape[0] // TILE) + local_tile
    unit_rows = min(half_rows, TILE)
    unit_count = query_part.shape[0] // unit_rows
    unit_pos = jnp.arange(unit_count, dtype=jnp.int32) * unit_rows
    source_head = unit_pos // half_rows
    first_row = source_head * (2 * half_rows) + kv_index * half_rows + unit_pos % half_rows
    unit_tile = first_row // TILE
    query_tile_ids = jnp.arange(tile_list.shape[0], dtype=jnp.int32)
    onehot = (unit_tile[:, None] == query_tile_ids[None, :]).astype(jnp.int32)
    unit_lists = jnp.sum(onehot[:, :, None] * full_tile[None, :, :], axis=1)
    block_units = math.gcd(unit_count, max(1, 512 // unit_rows))
    key_tiles = key_source.reshape(-1, TILE, feat_width)
    value_tiles = value_source.reshape(-1, TILE, feat_width)
    slot_count = unit_lists.shape[1]

    def unit_block(block_index):
        query_block = lax.dynamic_slice_in_dim(
            query_part, block_index * block_units * unit_rows, block_units * unit_rows, 0
        )
        query_block = query_block.reshape(block_units, unit_rows, heads_dev, DH)
        tile_ids = lax.dynamic_slice_in_dim(unit_lists, block_index * block_units, block_units, 0)
        key_block = key_tiles[tile_ids].reshape(block_units, slot_count * TILE, heads_dev, DH)
        value_block = value_tiles[tile_ids].reshape(block_units, slot_count * TILE, heads_dev, DH)
        scores = (
            jnp.einsum(
                "bqhd,bkhd->bhqk", query_block, key_block, preferred_element_type=jnp.float32
            )
            * inv_root
        )
        row_peak = jnp.max(scores, axis=-1)
        exponent = jnp.exp(scores - row_peak[..., None])
        row_total = jnp.sum(exponent, axis=-1)
        weight = exponent.astype(jnp.bfloat16)
        weighted = jnp.einsum(
            "bhqk,bkhd->bqhd", weight, value_block, preferred_element_type=jnp.float32
        )
        result = weighted / jnp.transpose(row_total, (0, 2, 1))[..., None]
        return result.astype(jnp.bfloat16).reshape(block_units * unit_rows, feat_width)

    block_rows = lax.map(unit_block, jnp.arange(unit_count // block_units, dtype=jnp.int32))
    normalized = block_rows.reshape(n_head, -1, feat_width)
    regrouped = lax.all_to_all(normalized, "head", split_axis=0, concat_axis=2, tiled=True)
    return regrouped.reshape(-1, HEADS * DH)


def fold_rows(block, op):
    return op(block.reshape(TILE // 8, 8, TILE), axis=0)


def score_pass(lists, q_ref, k_ref, s_next, a_next, n_sel, extra=None):
    query = q_ref[a_next]
    peak = None
    for j in range(n_sel):
        key = k_ref[lists[a_next, j]]
        s = lax.dot_general(key, query, (((1,), (1,)), ((), ())), preferred_element_type=jnp.float32)
        s_next[j * TILE : (j + 1) * TILE, :] = s
        part = fold_rows(s, jnp.max)
        peak = part if peak is None else jnp.maximum(peak, part)
        if extra is not None:
            extra(j)
    return jnp.max(peak, axis=0, keepdims=True)


def weights_phase(lists, q_ref, k_ref, p_ref, l_ref, s_a, s_b, n_q, n_sel):
    def both(a_next, s_next, a_now, s_now, peak):
        sums = []

        def weigh(j):
            rows = slice(j * TILE, (j + 1) * TILE)
            expo = jnp.exp2((s_now[rows, :] - peak) * EXP2_SCALE)
            p_ref[a_now, rows, :] = expo.astype(jnp.bfloat16)
            part = fold_rows(expo, jnp.sum)
            sums[:] = [part if not sums else sums[0] + part]

        peak_next = score_pass(lists, q_ref, k_ref, s_next, a_next, n_sel, weigh)
        total = jnp.sum(sums[0], axis=0, keepdims=True)
        l_ref[a_now] = jnp.broadcast_to(total, (8, TILE))
        return peak_next

    def pair(i, peak):
        first = 2 * i
        peak = both(first + 1, s_b, first, s_a, peak)
        return both(jnp.minimum(first + 2, n_q - 1), s_a, first + 1, s_b, peak)

    lax.fori_loop(0, n_q // 2, pair, score_pass(lists, q_ref, k_ref, s_a, 0, n_sel))


def turn_values(v_ref, vt_ref):
    def one(t, carry):
        vt_ref[t] = v_ref[t].T
        return carry

    lax.fori_loop(0, v_ref.shape[0], one, 0)


def output_tile(lists, vt_ref, p_ref, l_ref, a, n_sel):
    group = math.gcd(n_sel, 8)
    numer = jnp.zeros((DH, TILE), jnp.float32)
    for g in range(0, n_sel, group):
        value = jnp.concatenate([vt_ref[lists[a, g + j]] for j in range(group)], axis=1)
        weight = p_ref[a, g * TILE : (g + group) * TILE, :]
        numer += jnp.dot(value, weight, preferred_element_type=jnp.float32)
    return (numer / l_ref[a][:1, :]).T.astype(jnp.bfloat16)


def attend_kernel(lists, q_ref, k_ref, v_ref, o_ref, vt_ref, p_ref, l_ref, s_a, s_b):
    n_q, n_sel = lists.shape
    weights_phase(lists, q_ref, k_ref, p_ref, l_ref, s_a, s_b, n_q, n_sel)
    turn_values(v_ref, vt_ref)

    def one(a, carry):
        o_ref[a] = output_tile(lists, vt_ref, p_ref, l_ref, a, n_sel)
        return carry

    lax.fori_loop(0, n_q, one, 0)


def head_plan(queries, keys, values, tile_list):
    n_q, n_sel = tile_list.shape
    both = ("head", "kv")
    own_rows = lax.dynamic_slice_in_dim(queries, lax.axis_index("kv") * TILE, TILE, 0)
    query = lax.all_to_all(own_rows, both, split_axis=1, concat_axis=0, tiled=True)
    key = lax.all_to_all(keys, both, split_axis=1, concat_axis=0, tiled=True)
    value = lax.all_to_all(values, both, split_axis=1, concat_axis=0, tiled=True)
    query, key, value = (x.reshape(-1, TILE, DH) for x in (query, key, value))
    vmem = pl.BlockSpec(memory_space=pltpu.VMEM)
    out = pl.pallas_call(
        attend_kernel,
        out_shape=jax.ShapeDtypeStruct((n_q, TILE, DH), jnp.bfloat16),
        in_specs=[pl.BlockSpec(memory_space=pltpu.SMEM), vmem, vmem, vmem],
        out_specs=vmem,
        scratch_shapes=[
            pltpu.VMEM(value.shape, jnp.bfloat16),
            pltpu.VMEM((n_q, n_sel * TILE, TILE), jnp.bfloat16),
            pltpu.VMEM((n_q, 8, TILE), jnp.float32),
            pltpu.VMEM((n_sel * TILE, TILE), jnp.float32),
            pltpu.VMEM((n_sel * TILE, TILE), jnp.float32),
        ],
        compiler_params=pltpu.CompilerParams(vmem_limit_bytes=56 * 2**20),
    )(tile_list, query, key, value)
    return lax.all_to_all(out.reshape(n_q * TILE, DH), both, split_axis=0, concat_axis=1, tiled=True)


def local(queries, keys, values, tile_list):
    n_kv = lax.axis_size("kv")
    n_dev = lax.axis_size("head") * n_kv
    one_each = HEADS == n_dev and queries.shape[0] == n_kv * TILE and tile_list.shape[0] == n_dev
    if one_each and n_dev % 2 == 0 and keys.shape[0] % TILE == 0:
        return head_plan(queries, keys, values, tile_list)
    return general_plan(queries, keys, values, tile_list)


def solution(mesh):
    return jax.shard_map(
        local,
        mesh=mesh,
        in_specs=(
            P(("clip", "head"), None),
            P(("clip", "head", "kv"), None),
            P(("clip", "head", "kv"), None),
            P("clip", None),
        ),
        out_specs=P(("clip", "head", "kv"), None),
        check_vma=False,
    )
```

```python
import functools
import math

import jax
import jax.numpy as jnp
from jax import lax
from jax.experimental import pallas as pl
from jax.experimental.pallas import tpu as pltpu
from jax.sharding import PartitionSpec as P

HEADS = 32
DH = 128
TILE = 128
KTOK_DEV = 256
EXP2_SCALE = math.log2(math.e) / math.sqrt(DH)


def general_plan(queries, keys, values, tile_list):
    n_head = lax.axis_size("head")
    heads_dev = HEADS // n_head
    kv_index = lax.axis_index("kv")
    key_all, value_all = (
        lax.all_to_all(keys, "head", split_axis=1, concat_axis=0, tiled=True),
        lax.all_to_all(values, "head", split_axis=1, concat_axis=0, tiled=True),
    )
    tile_span = KTOK_DEV // TILE
    key_shard = tile_list // tile_span
    parity = key_shard % 2
    local_tile = key_shard // 2 * tile_span + tile_list % tile_span
    inv_root = 1.0 / jnp.sqrt(jnp.float32(DH))
    feat_width = key_all.shape[1]
    half_rows = queries.shape[0] // 2
    own_rows = lax.dynamic_slice_in_dim(queries, kv_index * half_rows, half_rows, 0)
    query_part = lax.all_to_all(own_rows, "head", split_axis=1, concat_axis=0, tiled=True)
    key_source, value_source = (
        lax.all_gather(key_all, "kv", axis=0, tiled=True),
        lax.all_gather(value_all, "kv", axis=0, tiled=True),
    )
    full_tile = parity * (key_all.shape[0] // TILE) + local_tile
    unit_rows = min(half_rows, TILE)
    unit_count = query_part.shape[0] // unit_rows
    unit_pos = jnp.arange(unit_count, dtype=jnp.int32) * unit_rows
    source_head = unit_pos // half_rows
    first_row = source_head * (2 * half_rows) + kv_index * half_rows + unit_pos % half_rows
    unit_tile = first_row // TILE
    query_tile_ids = jnp.arange(tile_list.shape[0], dtype=jnp.int32)
    onehot = (unit_tile[:, None] == query_tile_ids[None, :]).astype(jnp.int32)
    unit_lists = jnp.sum(onehot[:, :, None] * full_tile[None, :, :], axis=1)
    block_units = math.gcd(unit_count, max(1, 512 // unit_rows))
    key_tiles = key_source.reshape(-1, TILE, feat_width)
    value_tiles = value_source.reshape(-1, TILE, feat_width)
    slot_count = unit_lists.shape[1]

    def unit_block(block_index):
        query_block = lax.dynamic_slice_in_dim(
            query_part, block_index * block_units * unit_rows, block_units * unit_rows, 0
        )
        query_block = query_block.reshape(block_units, unit_rows, heads_dev, DH)
        tile_ids = lax.dynamic_slice_in_dim(unit_lists, block_index * block_units, block_units, 0)
        key_block = key_tiles[tile_ids].reshape(block_units, slot_count * TILE, heads_dev, DH)
        value_block = value_tiles[tile_ids].reshape(block_units, slot_count * TILE, heads_dev, DH)
        scores = (
            jnp.einsum(
                "bqhd,bkhd->bhqk", query_block, key_block, preferred_element_type=jnp.float32
            )
            * inv_root
        )
        row_peak = jnp.max(scores, axis=-1)
        exponent = jnp.exp(scores - row_peak[..., None])
        row_total = jnp.sum(exponent, axis=-1)
        weight = exponent.astype(jnp.bfloat16)
        weighted = jnp.einsum(
            "bhqk,bkhd->bqhd", weight, value_block, preferred_element_type=jnp.float32
        )
        result = weighted / jnp.transpose(row_total, (0, 2, 1))[..., None]
        return result.astype(jnp.bfloat16).reshape(block_units * unit_rows, feat_width)

    block_rows = lax.map(unit_block, jnp.arange(unit_count // block_units, dtype=jnp.int32))
    normalized = block_rows.reshape(n_head, -1, feat_width)
    regrouped = lax.all_to_all(normalized, "head", split_axis=0, concat_axis=2, tiled=True)
    return regrouped.reshape(-1, HEADS * DH)


def fold_rows(block, op):
    return op(block.reshape(TILE // 8, 8, TILE), axis=0)


def score_pass(lists, q_ref, k_ref, s_next, a_next, n_sel, extra=None):
    query = q_ref[a_next]
    peak = None
    for j in range(n_sel):
        key = k_ref[lists[a_next, j]]
        s = lax.dot_general(key, query, (((1,), (1,)), ((), ())), preferred_element_type=jnp.float32)
        s_next[j * TILE : (j + 1) * TILE, :] = s
        part = fold_rows(s, jnp.max)
        peak = part if peak is None else jnp.maximum(peak, part)
        if extra is not None:
            extra(j)
    return jnp.max(peak, axis=0, keepdims=True)


def weights_phase(lists, q_ref, k_ref, p_ref, l_ref, s_a, s_b, n_q, n_sel):
    def both(a_next, s_next, a_now, s_now, peak):
        sums = []

        def weigh(j):
            rows = slice(j * TILE, (j + 1) * TILE)
            expo = jnp.exp2((s_now[rows, :] - peak) * EXP2_SCALE)
            p_ref[a_now, rows, :] = expo.astype(jnp.bfloat16)
            part = fold_rows(expo, jnp.sum)
            sums[:] = [part if not sums else sums[0] + part]

        peak_next = score_pass(lists, q_ref, k_ref, s_next, a_next, n_sel, weigh)
        total = jnp.sum(sums[0], axis=0, keepdims=True)
        l_ref[a_now] = jnp.broadcast_to(total, (8, TILE))
        return peak_next

    def pair(i, peak):
        first = 2 * i
        peak = both(first + 1, s_b, first, s_a, peak)
        return both(jnp.minimum(first + 2, n_q - 1), s_a, first + 1, s_b, peak)

    lax.fori_loop(0, n_q // 2, pair, score_pass(lists, q_ref, k_ref, s_a, 0, n_sel))


def turn_values(v_ref, vt_ref):
    def one(t, carry):
        vt_ref[t] = v_ref[t].T
        return carry

    lax.fori_loop(0, v_ref.shape[0], one, 0)


def output_tile(lists, vt_ref, p_ref, l_ref, a, n_sel):
    group = math.gcd(n_sel, 8)
    numer = jnp.zeros((DH, TILE), jnp.float32)
    for g in range(0, n_sel, group):
        value = jnp.concatenate([vt_ref[lists[a, g + j]] for j in range(group)], axis=1)
        weight = p_ref[a, g * TILE : (g + group) * TILE, :]
        numer += jnp.dot(value, weight, preferred_element_type=jnp.float32)
    return (numer / l_ref[a][:1, :]).T.astype(jnp.bfloat16)


def fused_kernel(
    lists, q_hbm, k_hbm, v_hbm, o_hbm, q_ref, k_ref, v_ref, vt_ref, p_ref, l_ref, s_a, s_b, stage, send, recv, own
):
    n_q, n_sel = lists.shape
    n_kv = lax.axis_size("kv")
    n_dev = lax.axis_size("head") * n_kv
    kv = lax.axis_index("kv")
    me = lax.axis_index("head") * n_kv + kv
    per_dev = k_hbm.shape[0]

    def where(p):
        return {"head": p // n_kv, "kv": lax.rem(p, n_kv)}

    def columns(p):
        return pl.ds(pl.multiple_of(p * DH, DH), DH)

    barrier = pltpu.get_barrier_semaphore()

    def greet(i, carry):
        pl.semaphore_signal(
            barrier, inc=1, device_id=where(lax.rem(me + i, n_dev)), device_id_type=pl.DeviceIdType.MESH
        )
        return carry

    lax.fori_loop(1, n_dev, greet, 0)
    pl.semaphore_wait(barrier, n_dev - 1)

    def blocks(p):
        token = pl.ds(me * per_dev, per_dev)
        return (
            (q_hbm.at[pl.ds(kv, 1), :, columns(p)], q_ref.at[pl.ds(me, 1)]),
            (k_hbm.at[:, :, columns(p)], k_ref.at[token]),
            (v_hbm.at[:, :, columns(p)], v_ref.at[token]),
        )

    mine = [pltpu.make_async_copy(src, dst, own.at[c]) for c, (src, dst) in enumerate(blocks(me))]
    for copy in mine:
        copy.start()

    def push(kinds):
        def one(i, carry):
            p = lax.rem(me + i, n_dev)
            pairs = blocks(p)
            for c in kinds:
                pltpu.make_async_remote_copy(
                    src_ref=pairs[c][0],
                    dst_ref=pairs[c][1],
                    send_sem=send.at[c],
                    recv_sem=recv.at[c],
                    device_id=where(p),
                    device_id_type=pl.DeviceIdType.MESH,
                ).start()
            return carry

        lax.fori_loop(1, n_dev, one, 0)

    def take(buffer, count, sem):
        span = buffer.at[pl.ds(0, (n_dev - 1) * count)]
        pltpu.make_async_copy(span, span, sem).wait()

    push((0, 1))
    push((2,))
    take(q_ref, 1, recv.at[0])
    take(k_ref, per_dev, recv.at[1])
    mine[0].wait()
    mine[1].wait()
    weights_phase(lists, q_ref, k_ref, p_ref, l_ref, s_a, s_b, n_q, n_sel)
    take(v_ref, per_dev, recv.at[2])
    mine[2].wait()
    turn_values(v_ref, vt_ref)

    def one(i, carry):
        a = lax.rem(me + i, n_dev)
        stage[a] = output_tile(lists, vt_ref, p_ref, l_ref, a, n_sel)

        @pl.when(i < n_dev)
        def _():
            pltpu.make_async_remote_copy(
                src_ref=stage.at[a],
                dst_ref=o_hbm.at[:, columns(me)],
                send_sem=send.at[3],
                recv_sem=recv.at[3],
                device_id=where(a),
                device_id_type=pl.DeviceIdType.MESH,
            ).start()

        return carry

    lax.fori_loop(1, n_dev + 1, one, 0)
    last = pltpu.make_async_copy(stage.at[me], o_hbm.at[:, columns(me)], own.at[3])
    last.start()
    take(q_ref, 1, send.at[0])
    take(k_ref, per_dev, send.at[1])
    take(v_ref, per_dev, send.at[2])
    take(stage, 1, send.at[3])
    take(stage, 1, recv.at[3])
    last.wait()


def head_plan(queries, keys, values, tile_list):
    n_q, n_sel = tile_list.shape
    n_dev = lax.axis_size("head") * lax.axis_size("kv")
    queries, keys, values = (x.reshape(-1, TILE, HEADS * DH) for x in (queries, keys, values))
    k_tiles = n_dev * keys.shape[0]
    hbm = pl.BlockSpec(memory_space=pl.ANY)
    flops = 4 * n_q * n_sel * TILE * TILE * DH
    return pl.pallas_call(
        fused_kernel,
        out_shape=jax.ShapeDtypeStruct((TILE, HEADS * DH), jnp.bfloat16),
        in_specs=[pl.BlockSpec(memory_space=pltpu.SMEM), hbm, hbm, hbm],
        out_specs=hbm,
        scratch_shapes=[
            pltpu.VMEM((n_q, TILE, DH), jnp.bfloat16),
            pltpu.VMEM((k_tiles, TILE, DH), jnp.bfloat16),
            pltpu.VMEM((k_tiles, TILE, DH), jnp.bfloat16),
            pltpu.VMEM((k_tiles, DH, TILE), jnp.bfloat16),
            pltpu.VMEM((n_q, n_sel * TILE, TILE), jnp.bfloat16),
            pltpu.VMEM((n_q, 8, TILE), jnp.float32),
            pltpu.VMEM((n_sel * TILE, TILE), jnp.float32),
            pltpu.VMEM((n_sel * TILE, TILE), jnp.float32),
            pltpu.VMEM((n_q, TILE, DH), jnp.bfloat16),
            pltpu.SemaphoreType.DMA((4,)),
            pltpu.SemaphoreType.DMA((4,)),
            pltpu.SemaphoreType.DMA((4,)),
        ],
        compiler_params=pltpu.CompilerParams(
            collective_id=0, has_side_effects=True, vmem_limit_bytes=56 * 2**20
        ),
        cost_estimate=pl.CostEstimate(flops=flops, bytes_accessed=8 * keys.size, transcendentals=0),
    )(tile_list, queries, keys, values)


def local(queries, keys, values, tile_list):
    n_kv = lax.axis_size("kv")
    n_dev = lax.axis_size("head") * n_kv
    one_each = HEADS == n_dev and queries.shape[0] == n_kv * TILE and tile_list.shape[0] == n_dev
    if one_each and n_dev % 2 == 0 and keys.shape[0] % TILE == 0:
        return head_plan(queries, keys, values, tile_list)
    return general_plan(queries, keys, values, tile_list)


def solution(mesh):
    return jax.shard_map(
        local,
        mesh=mesh,
        in_specs=(
            P(("clip", "head"), None),
            P(("clip", "head", "kv"), None),
            P(("clip", "head", "kv"), None),
            P("clip", None),
        ),
        out_specs=P(("clip", "head", "kv"), None),
        check_vma=False,
    )
```

```python
import functools
import math

import jax
import jax.numpy as jnp
from jax import lax
from jax.experimental import pallas as pl
from jax.experimental.pallas import tpu as pltpu
from jax.sharding import PartitionSpec as P

HEADS = 32
DH = 128
TILE = 128
KTOK_DEV = 256
EXP2_SCALE = math.log2(math.e) / math.sqrt(DH)


def general_plan(queries, keys, values, tile_list):
    n_head = lax.axis_size("head")
    heads_dev = HEADS // n_head
    kv_index = lax.axis_index("kv")
    key_all, value_all = (
        lax.all_to_all(keys, "head", split_axis=1, concat_axis=0, tiled=True),
        lax.all_to_all(values, "head", split_axis=1, concat_axis=0, tiled=True),
    )
    tile_span = KTOK_DEV // TILE
    key_shard = tile_list // tile_span
    parity = key_shard % 2
    local_tile = key_shard // 2 * tile_span + tile_list % tile_span
    inv_root = 1.0 / jnp.sqrt(jnp.float32(DH))
    feat_width = key_all.shape[1]
    half_rows = queries.shape[0] // 2
    own_rows = lax.dynamic_slice_in_dim(queries, kv_index * half_rows, half_rows, 0)
    query_part = lax.all_to_all(own_rows, "head", split_axis=1, concat_axis=0, tiled=True)
    key_source, value_source = (
        lax.all_gather(key_all, "kv", axis=0, tiled=True),
        lax.all_gather(value_all, "kv", axis=0, tiled=True),
    )
    full_tile = parity * (key_all.shape[0] // TILE) + local_tile
    unit_rows = min(half_rows, TILE)
    unit_count = query_part.shape[0] // unit_rows
    unit_pos = jnp.arange(unit_count, dtype=jnp.int32) * unit_rows
    source_head = unit_pos // half_rows
    first_row = source_head * (2 * half_rows) + kv_index * half_rows + unit_pos % half_rows
    unit_tile = first_row // TILE
    query_tile_ids = jnp.arange(tile_list.shape[0], dtype=jnp.int32)
    onehot = (unit_tile[:, None] == query_tile_ids[None, :]).astype(jnp.int32)
    unit_lists = jnp.sum(onehot[:, :, None] * full_tile[None, :, :], axis=1)
    block_units = math.gcd(unit_count, max(1, 512 // unit_rows))
    key_tiles = key_source.reshape(-1, TILE, feat_width)
    value_tiles = value_source.reshape(-1, TILE, feat_width)
    slot_count = unit_lists.shape[1]

    def unit_block(block_index):
        query_block = lax.dynamic_slice_in_dim(
            query_part, block_index * block_units * unit_rows, block_units * unit_rows, 0
        )
        query_block = query_block.reshape(block_units, unit_rows, heads_dev, DH)
        tile_ids = lax.dynamic_slice_in_dim(unit_lists, block_index * block_units, block_units, 0)
        key_block = key_tiles[tile_ids].reshape(block_units, slot_count * TILE, heads_dev, DH)
        value_block = value_tiles[tile_ids].reshape(block_units, slot_count * TILE, heads_dev, DH)
        scores = (
            jnp.einsum(
                "bqhd,bkhd->bhqk", query_block, key_block, preferred_element_type=jnp.float32
            )
            * inv_root
        )
        row_peak = jnp.max(scores, axis=-1)
        exponent = jnp.exp(scores - row_peak[..., None])
        row_total = jnp.sum(exponent, axis=-1)
        weight = exponent.astype(jnp.bfloat16)
        weighted = jnp.einsum(
            "bhqk,bkhd->bqhd", weight, value_block, preferred_element_type=jnp.float32
        )
        result = weighted / jnp.transpose(row_total, (0, 2, 1))[..., None]
        return result.astype(jnp.bfloat16).reshape(block_units * unit_rows, feat_width)

    block_rows = lax.map(unit_block, jnp.arange(unit_count // block_units, dtype=jnp.int32))
    normalized = block_rows.reshape(n_head, -1, feat_width)
    regrouped = lax.all_to_all(normalized, "head", split_axis=0, concat_axis=2, tiled=True)
    return regrouped.reshape(-1, HEADS * DH)


def fold_rows(block, op):
    return op(block.reshape(TILE // 8, 8, TILE), axis=0)


def score_pass(lists, q_ref, k_ref, s_next, a_next, n_sel, extra=None):
    query = q_ref[a_next]
    peak = None
    for j in range(n_sel):
        key = k_ref[lists[a_next, j]]
        s = lax.dot_general(key, query, (((1,), (1,)), ((), ())), preferred_element_type=jnp.float32)
        s_next[j * TILE : (j + 1) * TILE, :] = s
        part = fold_rows(s, jnp.max)
        peak = part if peak is None else jnp.maximum(peak, part)
        if extra is not None:
            extra(j)
    return jnp.max(peak, axis=0, keepdims=True)


def weights_phase(lists, q_ref, k_ref, p_ref, l_ref, s_a, s_b, n_q, n_sel):
    def both(a_next, s_next, a_now, s_now, peak):
        sums = []

        def weigh(j):
            rows = slice(j * TILE, (j + 1) * TILE)
            expo = jnp.exp2((s_now[rows, :] - peak) * EXP2_SCALE)
            p_ref[a_now, rows, :] = expo.astype(jnp.bfloat16)
            part = fold_rows(expo, jnp.sum)
            sums[:] = [part if not sums else sums[0] + part]

        peak_next = score_pass(lists, q_ref, k_ref, s_next, a_next, n_sel, weigh)
        total = jnp.sum(sums[0], axis=0, keepdims=True)
        l_ref[a_now] = jnp.broadcast_to(total, (8, TILE))
        return peak_next

    def pair(i, peak):
        first = 2 * i
        peak = both(first + 1, s_b, first, s_a, peak)
        return both(jnp.minimum(first + 2, n_q - 1), s_a, first + 1, s_b, peak)

    lax.fori_loop(0, n_q // 2, pair, score_pass(lists, q_ref, k_ref, s_a, 0, n_sel))


def output_tile(lists, vt_ref, p_ref, l_ref, a, n_sel):
    group = math.gcd(n_sel, 8)
    numer = jnp.zeros((DH, TILE), jnp.float32)
    for g in range(0, n_sel, group):
        value = jnp.concatenate([vt_ref[lists[a, g + j]] for j in range(group)], axis=1)
        weight = p_ref[a, g * TILE : (g + group) * TILE, :]
        numer += jnp.dot(value, weight, preferred_element_type=jnp.float32)
    return (numer / l_ref[a][:1, :]).T.astype(jnp.bfloat16)


def fused_kernel(
    lists, q_hbm, k_hbm, v_hbm, o_hbm, q_ref, k_ref, v_raw, vt_out, vt_ref, p_ref, l_ref, s_a, s_b, stage, send, recv, own
):
    n_q, n_sel = lists.shape
    n_kv = lax.axis_size("kv")
    n_dev = lax.axis_size("head") * n_kv
    kv = lax.axis_index("kv")
    me = lax.axis_index("head") * n_kv + kv
    per_dev = k_hbm.shape[0]

    def where(p):
        return {"head": p // n_kv, "kv": lax.rem(p, n_kv)}

    def columns(p):
        return pl.ds(pl.multiple_of(p * DH, DH), DH)

    def partner(i):
        return lax.rem(me + i // 2 + i % 2 * (n_dev // 2), n_dev)

    load_values = pltpu.make_async_copy(v_hbm, v_raw, own.at[4])
    load_values.start()
    barrier = pltpu.get_barrier_semaphore()

    def greet(i, carry):
        pl.semaphore_signal(
            barrier, inc=1, device_id=where(lax.rem(me + i, n_dev)), device_id_type=pl.DeviceIdType.MESH
        )
        return carry

    lax.fori_loop(1, n_dev, greet, 0)
    pl.semaphore_wait(barrier, n_dev - 1)

    token = pl.ds(me * per_dev, per_dev)

    def blocks(p):
        return (
            (q_hbm.at[pl.ds(kv, 1), :, columns(p)], q_ref.at[pl.ds(me, 1)]),
            (k_hbm.at[:, :, columns(p)], k_ref.at[token]),
            (vt_out.at[p], vt_ref.at[token]),
        )

    mine = [pltpu.make_async_copy(src, dst, own.at[c]) for c, (src, dst) in enumerate(blocks(me))]

    def push(kinds):
        def one(i, carry):
            p = partner(i)
            pairs = blocks(p)
            for c in kinds:
                pltpu.make_async_remote_copy(
                    src_ref=pairs[c][0],
                    dst_ref=pairs[c][1],
                    send_sem=send.at[c],
                    recv_sem=recv.at[c],
                    device_id=where(p),
                    device_id_type=pl.DeviceIdType.MESH,
                ).start()
            return carry

        lax.fori_loop(1, n_dev, one, 0)

    def take(buffer, count, sem):
        span = buffer.at[pl.ds(0, (n_dev - 1) * count)]
        pltpu.make_async_copy(span, span, sem).wait()

    push((0, 1))
    mine[0].start()
    mine[1].start()
    load_values.wait()

    def turn(p, carry):
        for b in range(per_dev):
            vt_out[p, b] = v_raw[b, :, columns(p)].T
        return carry

    lax.fori_loop(0, n_dev, turn, 0)
    mine[2].start()
    take(q_ref, 1, send.at[0])
    take(k_ref, per_dev, send.at[1])
    push((2,))
    take(q_ref, 1, recv.at[0])
    take(k_ref, per_dev, recv.at[1])
    mine[0].wait()
    mine[1].wait()
    weights_phase(lists, q_ref, k_ref, p_ref, l_ref, s_a, s_b, n_q, n_sel)
    take(vt_ref, per_dev, recv.at[2])
    mine[2].wait()

    def one(i, carry):
        a = partner(i)
        stage[a] = output_tile(lists, vt_ref, p_ref, l_ref, a, n_sel)
        pltpu.make_async_remote_copy(
            src_ref=stage.at[a],
            dst_ref=o_hbm.at[:, columns(me)],
            send_sem=send.at[3],
            recv_sem=recv.at[3],
            device_id=where(a),
            device_id_type=pl.DeviceIdType.MESH,
        ).start()
        return carry

    lax.fori_loop(1, n_dev, one, 0)
    stage[me] = output_tile(lists, vt_ref, p_ref, l_ref, me, n_sel)
    last = pltpu.make_async_copy(stage.at[me], o_hbm.at[:, columns(me)], own.at[3])
    last.start()
    take(vt_ref, per_dev, send.at[2])
    take(stage, 1, send.at[3])
    take(stage, 1, recv.at[3])
    last.wait()


def head_plan(queries, keys, values, tile_list):
    n_q, n_sel = tile_list.shape
    n_dev = lax.axis_size("head") * lax.axis_size("kv")
    queries, keys, values = (x.reshape(-1, TILE, HEADS * DH) for x in (queries, keys, values))
    k_tiles = n_dev * keys.shape[0]
    hbm = pl.BlockSpec(memory_space=pl.ANY)
    flops = 4 * n_q * n_sel * TILE * TILE * DH
    return pl.pallas_call(
        fused_kernel,
        out_shape=jax.ShapeDtypeStruct((TILE, HEADS * DH), jnp.bfloat16),
        in_specs=[pl.BlockSpec(memory_space=pltpu.SMEM), hbm, hbm, hbm],
        out_specs=hbm,
        scratch_shapes=[
            pltpu.VMEM((n_q, TILE, DH), jnp.bfloat16),
            pltpu.VMEM((k_tiles, TILE, DH), jnp.bfloat16),
            pltpu.VMEM(values.shape, jnp.bfloat16),
            pltpu.VMEM((n_dev, values.shape[0], DH, TILE), jnp.bfloat16),
            pltpu.VMEM((k_tiles, DH, TILE), jnp.bfloat16),
            pltpu.VMEM((n_q, n_sel * TILE, TILE), jnp.bfloat16),
            pltpu.VMEM((n_q, 8, TILE), jnp.float32),
            pltpu.VMEM((n_sel * TILE, TILE), jnp.float32),
            pltpu.VMEM((n_sel * TILE, TILE), jnp.float32),
            pltpu.VMEM((n_q, TILE, DH), jnp.bfloat16),
            pltpu.SemaphoreType.DMA((4,)),
            pltpu.SemaphoreType.DMA((4,)),
            pltpu.SemaphoreType.DMA((5,)),
        ],
        compiler_params=pltpu.CompilerParams(
            collective_id=0, has_side_effects=True, vmem_limit_bytes=56 * 2**20
        ),
        cost_estimate=pl.CostEstimate(flops=flops, bytes_accessed=8 * keys.size, transcendentals=0),
    )(tile_list, queries, keys, values)


def local(queries, keys, values, tile_list):
    n_kv = lax.axis_size("kv")
    n_dev = lax.axis_size("head") * n_kv
    one_each = HEADS == n_dev and queries.shape[0] == n_kv * TILE and tile_list.shape[0] == n_dev
    if one_each and n_dev % 2 == 0 and keys.shape[0] % TILE == 0:
        return head_plan(queries, keys, values, tile_list)
    return general_plan(queries, keys, values, tile_list)


def solution(mesh):
    return jax.shard_map(
        local,
        mesh=mesh,
        in_specs=(
            P(("clip", "head"), None),
            P(("clip", "head", "kv"), None),
            P(("clip", "head", "kv"), None),
            P("clip", None),
        ),
        out_specs=P(("clip", "head", "kv"), None),
        check_vma=False,
    )
```

```python
import functools
import math

import jax
import jax.numpy as jnp
from jax import lax
from jax.experimental import pallas as pl
from jax.experimental.pallas import tpu as pltpu
from jax.sharding import PartitionSpec as P

HEADS = 32
DH = 128
TILE = 128
KTOK_DEV = 256
EXP2_SCALE = math.log2(math.e) / math.sqrt(DH)


def general_plan(queries, keys, values, tile_list):
    n_head = lax.axis_size("head")
    heads_dev = HEADS // n_head
    kv_index = lax.axis_index("kv")
    key_all, value_all = (
        lax.all_to_all(keys, "head", split_axis=1, concat_axis=0, tiled=True),
        lax.all_to_all(values, "head", split_axis=1, concat_axis=0, tiled=True),
    )
    tile_span = KTOK_DEV // TILE
    key_shard = tile_list // tile_span
    parity = key_shard % 2
    local_tile = key_shard // 2 * tile_span + tile_list % tile_span
    inv_root = 1.0 / jnp.sqrt(jnp.float32(DH))
    feat_width = key_all.shape[1]
    half_rows = queries.shape[0] // 2
    own_rows = lax.dynamic_slice_in_dim(queries, kv_index * half_rows, half_rows, 0)
    query_part = lax.all_to_all(own_rows, "head", split_axis=1, concat_axis=0, tiled=True)
    key_source, value_source = (
        lax.all_gather(key_all, "kv", axis=0, tiled=True),
        lax.all_gather(value_all, "kv", axis=0, tiled=True),
    )
    full_tile = parity * (key_all.shape[0] // TILE) + local_tile
    unit_rows = min(half_rows, TILE)
    unit_count = query_part.shape[0] // unit_rows
    unit_pos = jnp.arange(unit_count, dtype=jnp.int32) * unit_rows
    source_head = unit_pos // half_rows
    first_row = source_head * (2 * half_rows) + kv_index * half_rows + unit_pos % half_rows
    unit_tile = first_row // TILE
    query_tile_ids = jnp.arange(tile_list.shape[0], dtype=jnp.int32)
    onehot = (unit_tile[:, None] == query_tile_ids[None, :]).astype(jnp.int32)
    unit_lists = jnp.sum(onehot[:, :, None] * full_tile[None, :, :], axis=1)
    block_units = math.gcd(unit_count, max(1, 512 // unit_rows))
    key_tiles = key_source.reshape(-1, TILE, feat_width)
    value_tiles = value_source.reshape(-1, TILE, feat_width)
    slot_count = unit_lists.shape[1]

    def unit_block(block_index):
        query_block = lax.dynamic_slice_in_dim(
            query_part, block_index * block_units * unit_rows, block_units * unit_rows, 0
        )
        query_block = query_block.reshape(block_units, unit_rows, heads_dev, DH)
        tile_ids = lax.dynamic_slice_in_dim(unit_lists, block_index * block_units, block_units, 0)
        key_block = key_tiles[tile_ids].reshape(block_units, slot_count * TILE, heads_dev, DH)
        value_block = value_tiles[tile_ids].reshape(block_units, slot_count * TILE, heads_dev, DH)
        scores = (
            jnp.einsum(
                "bqhd,bkhd->bhqk", query_block, key_block, preferred_element_type=jnp.float32
            )
            * inv_root
        )
        row_peak = jnp.max(scores, axis=-1)
        exponent = jnp.exp(scores - row_peak[..., None])
        row_total = jnp.sum(exponent, axis=-1)
        weight = exponent.astype(jnp.bfloat16)
        weighted = jnp.einsum(
            "bhqk,bkhd->bqhd", weight, value_block, preferred_element_type=jnp.float32
        )
        result = weighted / jnp.transpose(row_total, (0, 2, 1))[..., None]
        return result.astype(jnp.bfloat16).reshape(block_units * unit_rows, feat_width)

    block_rows = lax.map(unit_block, jnp.arange(unit_count // block_units, dtype=jnp.int32))
    normalized = block_rows.reshape(n_head, -1, feat_width)
    regrouped = lax.all_to_all(normalized, "head", split_axis=0, concat_axis=2, tiled=True)
    return regrouped.reshape(-1, HEADS * DH)


def fold_rows(block, op):
    return op(block.reshape(TILE // 8, 8, TILE), axis=0)


def score_pass(lists, q_ref, k_ref, s_next, a_next, n_sel, extra=None):
    query = q_ref[a_next]
    peak = None
    for j in range(n_sel):
        key = k_ref[lists[a_next, j]]
        s = lax.dot_general(key, query, (((1,), (1,)), ((), ())), preferred_element_type=jnp.float32)
        s_next[j * TILE : (j + 1) * TILE, :] = s
        part = fold_rows(s, jnp.max)
        peak = part if peak is None else jnp.maximum(peak, part)
        if extra is not None:
            extra(j)
    return jnp.max(peak, axis=0, keepdims=True)


def weights_phase(lists, q_ref, k_ref, p_ref, l_ref, s_a, s_b, n_q, n_sel):
    def both(a_next, s_next, a_now, s_now, peak):
        sums = []

        def weigh(j):
            rows = slice(j * TILE, (j + 1) * TILE)
            expo = jnp.exp2((s_now[rows, :] - peak) * EXP2_SCALE)
            p_ref[a_now, rows, :] = expo.astype(jnp.bfloat16)
            part = fold_rows(expo, jnp.sum)
            sums[:] = [part if not sums else sums[0] + part]

        peak_next = score_pass(lists, q_ref, k_ref, s_next, a_next, n_sel, weigh)
        total = jnp.sum(sums[0], axis=0, keepdims=True)
        l_ref[a_now] = jnp.broadcast_to(total, (8, TILE))
        return peak_next

    def pair(i, peak):
        first = 2 * i
        peak = both(first + 1, s_b, first, s_a, peak)
        return both(jnp.minimum(first + 2, n_q - 1), s_a, first + 1, s_b, peak)

    lax.fori_loop(0, n_q // 2, pair, score_pass(lists, q_ref, k_ref, s_a, 0, n_sel))


def output_tile(lists, vt_ref, p_ref, l_ref, a, n_sel):
    group = math.gcd(n_sel, 8)
    numer = jnp.zeros((DH, TILE), jnp.float32)
    for g in range(0, n_sel, group):
        value = jnp.concatenate([vt_ref[lists[a, g + j]] for j in range(group)], axis=1)
        weight = p_ref[a, g * TILE : (g + group) * TILE, :]
        numer += jnp.dot(value, weight, preferred_element_type=jnp.float32)
    return (numer / l_ref[a][:1, :]).T.astype(jnp.bfloat16)


def fused_kernel(
    lists, q_hbm, k_hbm, v_hbm, o_hbm, q_ref, k_ref, q_out, k_out, v_raw, vt_out, vt_ref, p_ref, l_ref, s_a, s_b, stage, send, recv, own
):
    n_q, n_sel = lists.shape
    n_kv = lax.axis_size("kv")
    n_dev = lax.axis_size("head") * n_kv
    kv = lax.axis_index("kv")
    me = lax.axis_index("head") * n_kv + kv
    per_dev = k_hbm.shape[0]

    def where(p):
        return {"head": p // n_kv, "kv": lax.rem(p, n_kv)}

    def columns(p):
        return pl.ds(pl.multiple_of(p * DH, DH), DH)

    def partner(i):
        return lax.rem(me + i // 2 + i % 2 * (n_dev // 2), n_dev)

    def load(p, carry):
        pltpu.make_async_copy(q_hbm.at[kv, :, columns(p)], q_out.at[p], own.at[5]).start()
        pltpu.make_async_copy(k_hbm.at[:, :, columns(p)], k_out.at[p], own.at[6]).start()
        return carry

    lax.fori_loop(0, n_dev, load, 0)
    load_values = pltpu.make_async_copy(v_hbm, v_raw, own.at[4])
    load_values.start()
    barrier = pltpu.get_barrier_semaphore()

    def greet(i, carry):
        pl.semaphore_signal(
            barrier, inc=1, device_id=where(lax.rem(me + i, n_dev)), device_id_type=pl.DeviceIdType.MESH
        )
        return carry

    lax.fori_loop(1, n_dev, greet, 0)
    pl.semaphore_wait(barrier, n_dev - 1)

    token = pl.ds(me * per_dev, per_dev)

    def blocks(p):
        return (
            (q_out.at[p], q_ref.at[me]),
            (k_out.at[p], k_ref.at[token]),
            (vt_out.at[p], vt_ref.at[token]),
        )

    mine = [pltpu.make_async_copy(src, dst, own.at[c]) for c, (src, dst) in enumerate(blocks(me))]

    def push(kinds, first, end, k_send):
        def one(i, carry):
            p = partner(i)
            pairs = blocks(p)
            for c in kinds:
                pltpu.make_async_remote_copy(
                    src_ref=pairs[c][0],
                    dst_ref=pairs[c][1],
                    send_sem=send.at[k_send if c == 1 else c],
                    recv_sem=recv.at[c],
                    device_id=where(p),
                    device_id_type=pl.DeviceIdType.MESH,
                ).start()
            return carry

        lax.fori_loop(first, end, one, 0)

    def take(buffer, count, sem):
        span = buffer.at[pl.ds(0, count)]
        pltpu.make_async_copy(span, span, sem).wait()

    pltpu.make_async_copy(q_out, q_out, own.at[5]).wait()
    pltpu.make_async_copy(k_out, k_out, own.at[6]).wait()
    others = n_dev - 1
    early = others * 2 // 3
    push((0, 1), 1, early + 1, 1)
    push((0, 1), early + 1, n_dev, 4)
    mine[0].start()
    mine[1].start()
    load_values.wait()

    def turn(p, carry):
        for b in range(per_dev):
            vt_out[p, b] = v_raw[b, :, columns(p)].T
        return carry

    lax.fori_loop(0, n_dev, turn, 0)
    mine[2].start()
    take(k_ref, early * per_dev, send.at[1])
    push((2,), 1, n_dev, 1)
    take(q_ref, others, recv.at[0])
    take(k_ref, others * per_dev, recv.at[1])
    mine[0].wait()
    mine[1].wait()
    weights_phase(lists, q_ref, k_ref, p_ref, l_ref, s_a, s_b, n_q, n_sel)
    take(vt_ref, others * per_dev, recv.at[2])
    mine[2].wait()

    def one(i, carry):
        a = partner(i)
        stage[a] = output_tile(lists, vt_ref, p_ref, l_ref, a, n_sel)
        pltpu.make_async_remote_copy(
            src_ref=stage.at[a],
            dst_ref=o_hbm.at[:, columns(me)],
            send_sem=send.at[3],
            recv_sem=recv.at[3],
            device_id=where(a),
            device_id_type=pl.DeviceIdType.MESH,
        ).start()
        return carry

    lax.fori_loop(1, n_dev, one, 0)
    stage[me] = output_tile(lists, vt_ref, p_ref, l_ref, me, n_sel)
    last = pltpu.make_async_copy(stage.at[me], o_hbm.at[:, columns(me)], own.at[3])
    last.start()
    take(q_ref, others, send.at[0])
    take(k_ref, (others - early) * per_dev, send.at[4])
    take(vt_ref, others * per_dev, send.at[2])
    take(stage, others, send.at[3])
    take(stage, others, recv.at[3])
    last.wait()


def head_plan(queries, keys, values, tile_list):
    n_q, n_sel = tile_list.shape
    n_dev = lax.axis_size("head") * lax.axis_size("kv")
    queries, keys, values = (x.reshape(-1, TILE, HEADS * DH) for x in (queries, keys, values))
    k_tiles = n_dev * keys.shape[0]
    hbm = pl.BlockSpec(memory_space=pl.ANY)
    flops = 4 * n_q * n_sel * TILE * TILE * DH
    return pl.pallas_call(
        fused_kernel,
        out_shape=jax.ShapeDtypeStruct((TILE, HEADS * DH), jnp.bfloat16),
        in_specs=[pl.BlockSpec(memory_space=pltpu.SMEM), hbm, hbm, hbm],
        out_specs=hbm,
        scratch_shapes=[
            pltpu.VMEM((n_q, TILE, DH), jnp.bfloat16),
            pltpu.VMEM((k_tiles, TILE, DH), jnp.bfloat16),
            pltpu.VMEM((n_dev, TILE, DH), jnp.bfloat16),
            pltpu.VMEM((n_dev, keys.shape[0], TILE, DH), jnp.bfloat16),
            pltpu.VMEM(values.shape, jnp.bfloat16),
            pltpu.VMEM((n_dev, values.shape[0], DH, TILE), jnp.bfloat16),
            pltpu.VMEM((k_tiles, DH, TILE), jnp.bfloat16),
            pltpu.VMEM((n_q, n_sel * TILE, TILE), jnp.bfloat16),
            pltpu.VMEM((n_q, 8, TILE), jnp.float32),
            pltpu.VMEM((n_sel * TILE, TILE), jnp.float32),
            pltpu.VMEM((n_sel * TILE, TILE), jnp.float32),
            pltpu.VMEM((n_q, TILE, DH), jnp.bfloat16),
            pltpu.SemaphoreType.DMA((5,)),
            pltpu.SemaphoreType.DMA((4,)),
            pltpu.SemaphoreType.DMA((7,)),
        ],
        compiler_params=pltpu.CompilerParams(
            collective_id=0, has_side_effects=True, vmem_limit_bytes=56 * 2**20
        ),
        cost_estimate=pl.CostEstimate(flops=flops, bytes_accessed=8 * keys.size, transcendentals=0),
    )(tile_list, queries, keys, values)


def local(queries, keys, values, tile_list):
    n_kv = lax.axis_size("kv")
    n_dev = lax.axis_size("head") * n_kv
    one_each = HEADS == n_dev and queries.shape[0] == n_kv * TILE and tile_list.shape[0] == n_dev
    if one_each and n_dev % 2 == 0 and keys.shape[0] % TILE == 0:
        return head_plan(queries, keys, values, tile_list)
    return general_plan(queries, keys, values, tile_list)


def solution(mesh):
    return jax.shard_map(
        local,
        mesh=mesh,
        in_specs=(
            P(("clip", "head"), None),
            P(("clip", "head", "kv"), None),
            P(("clip", "head", "kv"), None),
            P("clip", None),
        ),
        out_specs=P(("clip", "head", "kv"), None),
        check_vma=False,
    )
```

```python
import functools
import math

import jax
import jax.numpy as jnp
from jax import lax
from jax.experimental import pallas as pl
from jax.experimental.pallas import tpu as pltpu
from jax.sharding import PartitionSpec as P

HEADS = 32
DH = 128
TILE = 128
KTOK_DEV = 256
EXP2_SCALE = math.log2(math.e) / math.sqrt(DH)


def general_plan(queries, keys, values, tile_list):
    n_head = lax.axis_size("head")
    heads_dev = HEADS // n_head
    kv_index = lax.axis_index("kv")
    key_all, value_all = (
        lax.all_to_all(keys, "head", split_axis=1, concat_axis=0, tiled=True),
        lax.all_to_all(values, "head", split_axis=1, concat_axis=0, tiled=True),
    )
    tile_span = KTOK_DEV // TILE
    key_shard = tile_list // tile_span
    parity = key_shard % 2
    local_tile = key_shard // 2 * tile_span + tile_list % tile_span
    inv_root = 1.0 / jnp.sqrt(jnp.float32(DH))
    feat_width = key_all.shape[1]
    half_rows = queries.shape[0] // 2
    own_rows = lax.dynamic_slice_in_dim(queries, kv_index * half_rows, half_rows, 0)
    query_part = lax.all_to_all(own_rows, "head", split_axis=1, concat_axis=0, tiled=True)
    key_source, value_source = (
        lax.all_gather(key_all, "kv", axis=0, tiled=True),
        lax.all_gather(value_all, "kv", axis=0, tiled=True),
    )
    full_tile = parity * (key_all.shape[0] // TILE) + local_tile
    unit_rows = min(half_rows, TILE)
    unit_count = query_part.shape[0] // unit_rows
    unit_pos = jnp.arange(unit_count, dtype=jnp.int32) * unit_rows
    source_head = unit_pos // half_rows
    first_row = source_head * (2 * half_rows) + kv_index * half_rows + unit_pos % half_rows
    unit_tile = first_row // TILE
    query_tile_ids = jnp.arange(tile_list.shape[0], dtype=jnp.int32)
    onehot = (unit_tile[:, None] == query_tile_ids[None, :]).astype(jnp.int32)
    unit_lists = jnp.sum(onehot[:, :, None] * full_tile[None, :, :], axis=1)
    block_units = math.gcd(unit_count, max(1, 512 // unit_rows))
    key_tiles = key_source.reshape(-1, TILE, feat_width)
    value_tiles = value_source.reshape(-1, TILE, feat_width)
    slot_count = unit_lists.shape[1]

    def unit_block(block_index):
        query_block = lax.dynamic_slice_in_dim(
            query_part, block_index * block_units * unit_rows, block_units * unit_rows, 0
        )
        query_block = query_block.reshape(block_units, unit_rows, heads_dev, DH)
        tile_ids = lax.dynamic_slice_in_dim(unit_lists, block_index * block_units, block_units, 0)
        key_block = key_tiles[tile_ids].reshape(block_units, slot_count * TILE, heads_dev, DH)
        value_block = value_tiles[tile_ids].reshape(block_units, slot_count * TILE, heads_dev, DH)
        scores = (
            jnp.einsum(
                "bqhd,bkhd->bhqk", query_block, key_block, preferred_element_type=jnp.float32
            )
            * inv_root
        )
        row_peak = jnp.max(scores, axis=-1)
        exponent = jnp.exp(scores - row_peak[..., None])
        row_total = jnp.sum(exponent, axis=-1)
        weight = exponent.astype(jnp.bfloat16)
        weighted = jnp.einsum(
            "bhqk,bkhd->bqhd", weight, value_block, preferred_element_type=jnp.float32
        )
        result = weighted / jnp.transpose(row_total, (0, 2, 1))[..., None]
        return result.astype(jnp.bfloat16).reshape(block_units * unit_rows, feat_width)

    block_rows = lax.map(unit_block, jnp.arange(unit_count // block_units, dtype=jnp.int32))
    normalized = block_rows.reshape(n_head, -1, feat_width)
    regrouped = lax.all_to_all(normalized, "head", split_axis=0, concat_axis=2, tiled=True)
    return regrouped.reshape(-1, HEADS * DH)


def fold_rows(block, op):
    return op(block.reshape(-1, 8, TILE), axis=0)


def score_pass(lists, q_ref, k_ref, s_next, a_next, n_sel, extra=None):
    query = q_ref[a_next]
    peak = None
    group = math.gcd(n_sel, 4)
    for g in range(0, n_sel, group):
        key = jnp.concatenate([k_ref[lists[a_next, g + j]] for j in range(group)], axis=0)
        s = lax.dot_general(key, query, (((1,), (1,)), ((), ())), preferred_element_type=jnp.float32)
        s_next[g * TILE : (g + group) * TILE, :] = s
        part = fold_rows(s, jnp.max)
        peak = part if peak is None else jnp.maximum(peak, part)
        if extra is not None:
            for j in range(group):
                extra(g + j)
    return jnp.max(peak, axis=0, keepdims=True)


def weights_phase(lists, q_ref, k_ref, p_ref, l_ref, s_a, s_b, n_q, n_sel):
    def both(a_next, s_next, a_now, s_now, peak):
        sums = []

        def weigh(j):
            rows = slice(j * TILE, (j + 1) * TILE)
            expo = jnp.exp2((s_now[rows, :] - peak) * EXP2_SCALE)
            p_ref[a_now, rows, :] = expo.astype(jnp.bfloat16)
            part = fold_rows(expo, jnp.sum)
            sums[:] = [part if not sums else sums[0] + part]

        peak_next = score_pass(lists, q_ref, k_ref, s_next, a_next, n_sel, weigh)
        total = jnp.sum(sums[0], axis=0, keepdims=True)
        l_ref[a_now] = jnp.broadcast_to(total, (8, TILE))
        return peak_next

    def pair(i, peak):
        first = 2 * i
        peak = both(first + 1, s_b, first, s_a, peak)
        return both(jnp.minimum(first + 2, n_q - 1), s_a, first + 1, s_b, peak)

    lax.fori_loop(0, n_q // 2, pair, score_pass(lists, q_ref, k_ref, s_a, 0, n_sel))


def output_tile(lists, vt_ref, p_ref, l_ref, a, n_sel):
    group = math.gcd(n_sel, 8)
    numer = jnp.zeros((DH, TILE), jnp.float32)
    for g in range(0, n_sel, group):
        value = jnp.concatenate([vt_ref[lists[a, g + j]] for j in range(group)], axis=1)
        weight = p_ref[a, g * TILE : (g + group) * TILE, :]
        numer += jnp.dot(value, weight, preferred_element_type=jnp.float32)
    return (numer / l_ref[a][:1, :]).T.astype(jnp.bfloat16)


def fused_kernel(
    lists, q_hbm, k_hbm, v_hbm, o_hbm, q_ref, k_ref, q_out, k_out, v_raw, vt_out, vt_ref, p_ref, l_ref, s_a, s_b, stage, send, recv, own
):
    n_q, n_sel = lists.shape
    n_kv = lax.axis_size("kv")
    n_dev = lax.axis_size("head") * n_kv
    kv = lax.axis_index("kv")
    me = lax.axis_index("head") * n_kv + kv
    per_dev = k_hbm.shape[0]

    def where(p):
        return {"head": p // n_kv, "kv": lax.rem(p, n_kv)}

    def columns(p):
        return pl.ds(pl.multiple_of(p * DH, DH), DH)

    def partner(i):
        return lax.rem(me + i // 2 + i % 2 * (n_dev // 2), n_dev)

    def load(p, carry):
        pltpu.make_async_copy(q_hbm.at[kv, :, columns(p)], q_out.at[p], own.at[5]).start()
        pltpu.make_async_copy(k_hbm.at[:, :, columns(p)], k_out.at[p], own.at[6]).start()
        return carry

    lax.fori_loop(0, n_dev, load, 0)
    load_values = pltpu.make_async_copy(v_hbm, v_raw, own.at[4])
    load_values.start()
    barrier = pltpu.get_barrier_semaphore()

    def greet(i, carry):
        pl.semaphore_signal(
            barrier, inc=1, device_id=where(lax.rem(me + i, n_dev)), device_id_type=pl.DeviceIdType.MESH
        )
        return carry

    lax.fori_loop(1, n_dev, greet, 0)
    pl.semaphore_wait(barrier, n_dev - 1)

    token = pl.ds(me * per_dev, per_dev)

    def blocks(p):
        return (
            (q_out.at[p], q_ref.at[me]),
            (k_out.at[p], k_ref.at[token]),
            (vt_out.at[p], vt_ref.at[token]),
        )

    mine = [pltpu.make_async_copy(src, dst, own.at[c]) for c, (src, dst) in enumerate(blocks(me))]

    def push(kinds, first, end, k_send):
        def one(i, carry):
            p = partner(i)
            pairs = blocks(p)
            for c in kinds:
                pltpu.make_async_remote_copy(
                    src_ref=pairs[c][0],
                    dst_ref=pairs[c][1],
                    send_sem=send.at[k_send if c == 1 else c],
                    recv_sem=recv.at[c],
                    device_id=where(p),
                    device_id_type=pl.DeviceIdType.MESH,
                ).start()
            return carry

        lax.fori_loop(first, end, one, 0)

    def take(buffer, count, sem):
        span = buffer.at[pl.ds(0, count)]
        pltpu.make_async_copy(span, span, sem).wait()

    pltpu.make_async_copy(q_out, q_out, own.at[5]).wait()
    pltpu.make_async_copy(k_out, k_out, own.at[6]).wait()
    others = n_dev - 1
    early = others * 2 // 3
    push((0, 1), 1, early + 1, 1)
    push((0, 1), early + 1, n_dev, 4)
    mine[0].start()
    mine[1].start()
    load_values.wait()

    def turn(p, carry):
        for b in range(per_dev):
            vt_out[p, b] = v_raw[b, :, columns(p)].T
        return carry

    lax.fori_loop(0, n_dev, turn, 0)
    mine[2].start()
    take(k_ref, early * per_dev, send.at[1])
    push((2,), 1, n_dev, 1)
    take(q_ref, others, recv.at[0])
    take(k_ref, others * per_dev, recv.at[1])
    mine[0].wait()
    mine[1].wait()
    weights_phase(lists, q_ref, k_ref, p_ref, l_ref, s_a, s_b, n_q, n_sel)
    take(vt_ref, others * per_dev, recv.at[2])
    mine[2].wait()

    def one(i, carry):
        a = partner(i)
        stage[a] = output_tile(lists, vt_ref, p_ref, l_ref, a, n_sel)
        pltpu.make_async_remote_copy(
            src_ref=stage.at[a],
            dst_ref=o_hbm.at[:, columns(me)],
            send_sem=send.at[3],
            recv_sem=recv.at[3],
            device_id=where(a),
            device_id_type=pl.DeviceIdType.MESH,
        ).start()
        return carry

    lax.fori_loop(1, n_dev, one, 0)
    stage[me] = output_tile(lists, vt_ref, p_ref, l_ref, me, n_sel)
    last = pltpu.make_async_copy(stage.at[me], o_hbm.at[:, columns(me)], own.at[3])
    last.start()
    take(q_ref, others, send.at[0])
    take(k_ref, (others - early) * per_dev, send.at[4])
    take(vt_ref, others * per_dev, send.at[2])
    take(stage, others, send.at[3])
    take(stage, others, recv.at[3])
    last.wait()


def head_plan(queries, keys, values, tile_list):
    n_q, n_sel = tile_list.shape
    n_dev = lax.axis_size("head") * lax.axis_size("kv")
    queries, keys, values = (x.reshape(-1, TILE, HEADS * DH) for x in (queries, keys, values))
    k_tiles = n_dev * keys.shape[0]
    hbm = pl.BlockSpec(memory_space=pl.ANY)
    flops = 4 * n_q * n_sel * TILE * TILE * DH
    return pl.pallas_call(
        fused_kernel,
        out_shape=jax.ShapeDtypeStruct((TILE, HEADS * DH), jnp.bfloat16),
        in_specs=[pl.BlockSpec(memory_space=pltpu.SMEM), hbm, hbm, hbm],
        out_specs=hbm,
        scratch_shapes=[
            pltpu.VMEM((n_q, TILE, DH), jnp.bfloat16),
            pltpu.VMEM((k_tiles, TILE, DH), jnp.bfloat16),
            pltpu.VMEM((n_dev, TILE, DH), jnp.bfloat16),
            pltpu.VMEM((n_dev, keys.shape[0], TILE, DH), jnp.bfloat16),
            pltpu.VMEM(values.shape, jnp.bfloat16),
            pltpu.VMEM((n_dev, values.shape[0], DH, TILE), jnp.bfloat16),
            pltpu.VMEM((k_tiles, DH, TILE), jnp.bfloat16),
            pltpu.VMEM((n_q, n_sel * TILE, TILE), jnp.bfloat16),
            pltpu.VMEM((n_q, 8, TILE), jnp.float32),
            pltpu.VMEM((n_sel * TILE, TILE), jnp.float32),
            pltpu.VMEM((n_sel * TILE, TILE), jnp.float32),
            pltpu.VMEM((n_q, TILE, DH), jnp.bfloat16),
            pltpu.SemaphoreType.DMA((5,)),
            pltpu.SemaphoreType.DMA((4,)),
            pltpu.SemaphoreType.DMA((7,)),
        ],
        compiler_params=pltpu.CompilerParams(
            collective_id=0, has_side_effects=True, vmem_limit_bytes=56 * 2**20
        ),
        cost_estimate=pl.CostEstimate(flops=flops, bytes_accessed=8 * keys.size, transcendentals=0),
    )(tile_list, queries, keys, values)


def local(queries, keys, values, tile_list):
    n_kv = lax.axis_size("kv")
    n_dev = lax.axis_size("head") * n_kv
    one_each = HEADS == n_dev and queries.shape[0] == n_kv * TILE and tile_list.shape[0] == n_dev
    if one_each and n_dev % 2 == 0 and keys.shape[0] % TILE == 0:
        return head_plan(queries, keys, values, tile_list)
    return general_plan(queries, keys, values, tile_list)


def solution(mesh):
    return jax.shard_map(
        local,
        mesh=mesh,
        in_specs=(
            P(("clip", "head"), None),
            P(("clip", "head", "kv"), None),
            P(("clip", "head", "kv"), None),
            P("clip", None),
        ),
        out_specs=P(("clip", "head", "kv"), None),
        check_vma=False,
    )
```
